256 devices in a mesh: ctx: 32 (over z, x), head: 8 (over y, core).
Axes of the slice: x: 4, y: 4, z: 8, core: 2. Of those that a mesh axis runs over, the one named last changes fastest.
Arguments:
- queries: bfloat16 [8192, 4096], P('ctx', 'head'), may hold values from -6 to 6
- keys: bfloat16 [8192, 4096], P('ctx', 'head'), may hold values from -6 to 6
- values: bfloat16 [8192, 4096], P('ctx', 'head'), may hold values from -6 to 6
- tan_queries: bfloat16 [8192, 4096], P('ctx', 'head'), may hold values from -6 to 6
- tan_keys: bfloat16 [8192, 4096], P('ctx', 'head'), may hold values from -6 to 6
- tan_values: bfloat16 [8192, 4096], P('ctx', 'head'), may hold values from -6 to 6
- w_out: bfloat16 [4096, 4096], P('head'), may hold values from -0.125 to 0.125
Outputs:
- mixed: bfloat16 [4096, 8192], P('head', 'ctx')
- tangent_mixed: bfloat16 [4096, 8192], P('head', 'ctx')
The draws below stay inside these ranges and needn't reach their ends.
All inputs are finite; a program needn't handle non-finite values.
Results may differ from the reference program's by a relative error of at most 0.022.
Values may be sent and summed in bfloat16 or wider, within the bound.
No kernel may reach another device: no remote copies, remote signals or barrier semaphores. Data moves between devices by JAX's collectives and lax.ppermute only.
A program may use at most 128 MiB of HBM per device.

```python
import math
import jax
import jax.numpy as jnp
from jax import lax

D = 4096
HEADS = 32
HD = 128
BLOCK = 128
TOKENS = 8192
N_HEAD = 8


def structure(key):
    block_count = TOKENS // BLOCK
    scale_count = block_count.bit_length()
    position = jnp.arange(TOKENS) // BLOCK
    total = jnp.zeros((TOKENS, D), jnp.float32)
    for depth_index in range(scale_count):
        table = jax.random.normal(jax.random.fold_in(key, depth_index + 100), (block_count >> depth_index, D), jnp.float32)
        total = total + table[position >> depth_index]
    return total / math.sqrt(scale_count)


def layered(key, rough):
    return jnp.clip(structure(key) + rough, -6.0, 6.0)


def draw_queries(key, part):
    key = jax.random.fold_in(key, 11)
    coarse = 2.0 * structure(jax.random.fold_in(key, 5))
    base = coarse + 0.5 * jax.random.normal(key, (TOKENS, D), jnp.float32)
    return jnp.clip(base, -6.0, 6.0).astype(jnp.bfloat16)


def draw_keys(key, part):
    key = jax.random.fold_in(key, 12)
    coarse = 2.0 * structure(jax.random.fold_in(key, 5))
    base = coarse + 0.5 * jax.random.normal(key, (TOKENS, D), jnp.float32)
    return jnp.clip(base, -6.0, 6.0).astype(jnp.bfloat16)


def draw_values(key, part):
    key = jax.random.fold_in(key, 21)
    rough = 0.7 * jax.random.normal(key, (TOKENS, D), jnp.float32)
    return layered(jax.random.fold_in(key, 5), rough).astype(jnp.bfloat16)


def draw_tan_values(key, part):
    key = jax.random.fold_in(key, 22)
    rough = 0.7 * jax.random.normal(key, (TOKENS, D), jnp.float32)
    return layered(jax.random.fold_in(key, 5), rough).astype(jnp.bfloat16)


def with_spikes(entries, key, source, target, blocks, factor):
    def block_of(dim):
        return (jnp.arange(entries.shape[dim]) // (entries.shape[dim] // blocks)).reshape((-1,) + (1,) * (entries.ndim - 1 - dim))

    near = jax.random.permutation(key, blocks)[block_of(target)]
    far = (block_of(target) + blocks // 2) % blocks
    return jnp.where((block_of(source) == near) | (block_of(source) == far), factor * entries, entries)


def shard_levels(own_key, extent, cuts, smallest, largest):
    def one(axis_at, blocks):
        heights = jax.random.uniform(jax.random.fold_in(jax.random.fold_in(own_key, 6), axis_at), (blocks,), jnp.float32, smallest / len(cuts), largest / len(cuts))
        return jnp.repeat(jnp.exp(heights), extent[axis_at] // blocks).reshape((-1,) + (1,) * (len(extent) - axis_at - 1))

    factor_of = one(*cuts[0])
    for cut in cuts[1:]:
        factor_of = factor_of * one(*cut)
    return factor_of


def scatter_about(rng, extent, scale, most, cuts=(), kind=jnp.bfloat16):
    values = scale * jax.random.normal(rng, extent, jnp.float32)
    if cuts:
        values = values * shard_levels(rng, extent, cuts, -0.22, 0.18)
    return jnp.clip(values, -most, most).astype(kind)


def noise_with(stream_key, extent, scale, reach, cuts, heavy, kind=jnp.bfloat16):
    entries = scale * jax.random.normal(stream_key, extent, jnp.float32)
    if cuts:
        entries = entries * shard_levels(stream_key, extent, cuts, -0.22, 0.18)
    return jnp.clip(with_spikes(entries, jax.random.fold_in(stream_key, 3), *heavy), -reach, reach).astype(kind)


def setup_inputs(seed: int = 0) -> dict:
    key_of = jax.random.split(jax.random.key(seed), 8)
    queries = draw_queries(jax.random.fold_in(key_of[7], 71), 0)
    keys = draw_keys(jax.random.fold_in(key_of[7], 71), 0)
    values = draw_values(jax.random.fold_in(key_of[7], 71), 0)
    tan_queries = scatter_about(key_of[3], (TOKENS, D), 1.0, 6.0, ((0, 32), (1, 8)))
    tan_keys = scatter_about(key_of[4], (TOKENS, D), 1.0, 6.0, ((0, 32), (1, 8)))
    tan_values = draw_tan_values(jax.random.fold_in(key_of[7], 71), 0)
    w_out = noise_with(key_of[6], (D, D), D ** -0.5, 0.125, ((0, 8),), (0, 1, 8, 2.0))
    return dict(queries=queries, keys=keys, values=values, tan_queries=tan_queries, tan_keys=tan_keys, tan_values=tan_values, w_out=w_out)


MASKED_SCORE = -1e+30
LOG_TWO = math.log(2.0)

def pool_pairs(array):
    row_count = array.shape[-2]
    paired = array.astype(jnp.float32).reshape(array.shape[:-2] + (row_count // 2, 2, array.shape[-1]))
    return (0.5 * (paired[..., 0, :] + paired[..., 1, :])).astype(jnp.bfloat16)

def level_terms(queries, keys, values, tan_q, tan_k, tan_v, offset, allowed):
    scale = 1.0 / math.sqrt(queries.shape[-1])
    form = '...qd,...kd->...qk'
    queries = queries.astype(jnp.float32)
    keys = keys.astype(jnp.float32)
    scores = jnp.einsum(form, queries, keys) * scale + offset
    slopes = (jnp.einsum(form, tan_q.astype(jnp.float32), keys) + jnp.einsum(form, queries, tan_k.astype(jnp.float32))) * scale
    if allowed is not None:
        scores = jnp.where(allowed, scores, MASKED_SCORE)
    top = lax.optimization_barrier(jnp.max(scores, axis=-1))
    probs = jnp.exp(scores - top[..., None])
    moved32 = probs * slopes
    weights = probs.astype(jnp.bfloat16).astype(jnp.float32)
    moved = moved32.astype(jnp.bfloat16).astype(jnp.float32)
    mixing = '...qk,...kd->...qd'
    num = jnp.einsum(mixing, weights, values.astype(jnp.float32))
    acc = jnp.einsum(mixing, moved, values.astype(jnp.float32)) + jnp.einsum(mixing, weights, tan_v.astype(jnp.float32))
    return (top, lax.optimization_barrier(jnp.sum(probs, axis=-1)), num, acc, lax.optimization_barrier(jnp.sum(moved32, axis=-1)))

def flatten(stats, lead, row_count, width):
    top, den, num, acc, curv = stats
    flat = lead + (row_count,)
    return (top.reshape(flat), den.reshape(flat), num.reshape(flat + (width,)), acc.reshape(flat + (width,)), curv.reshape(flat))

def leaf_terms(queries, keys, values, tan_q, tan_k, tan_v):
    lead = queries.shape[:-2]
    row_count = queries.shape[-2]
    width = queries.shape[-1]
    block_count = row_count // BLOCK

    def blocks(array):
        return array.reshape(lead + (block_count, BLOCK, width))

    def widen(array):
        tiled = blocks(array)
        return jnp.concatenate([jnp.roll(tiled, 1, axis=-3), tiled], axis=-2)
    odd_blocks = jnp.arange(block_count) % 2 == 1
    earlier = jnp.broadcast_to(odd_blocks[:, None, None], (block_count, BLOCK, BLOCK))
    causal = jnp.broadcast_to(jnp.arange(BLOCK)[:, None] >= jnp.arange(BLOCK)[None, :], (block_count, BLOCK, BLOCK))
    allowed = jnp.concatenate([earlier, causal], axis=-1)
    stats = level_terms(blocks(queries), widen(keys), widen(values), blocks(tan_q), widen(tan_k), widen(tan_v), 0.0, allowed)
    return flatten(stats, lead, row_count, width)

def pair_terms(arrays, level_num):
    queries, keys, values, tan_q, tan_k, tan_v = arrays
    lead = queries.shape[:-2]
    row_count = queries.shape[-2]
    width = queries.shape[-1]
    block_count = row_count // BLOCK

    def blocks(array):
        return array.reshape(lead + (block_count, BLOCK, width))

    def before(array):
        return jnp.roll(blocks(array), 1, axis=-3)
    stats = level_terms(blocks(queries), before(keys), before(values), blocks(tan_q), before(tan_k), before(tan_v), level_num * LOG_TWO, None)
    odd_blocks = (jnp.arange(block_count) % 2 == 1)[:, None]
    top = jnp.where(odd_blocks, stats[0], MASKED_SCORE)
    return flatten((top,) + stats[1:], lead, row_count, width)

def expand(stats, factor):
    top, den, num, acc, curv = stats
    return (jnp.repeat(top, factor, axis=-1), jnp.repeat(den, factor, axis=-1), jnp.repeat(num, factor, axis=-2), jnp.repeat(acc, factor, axis=-2), jnp.repeat(curv, factor, axis=-1))

def merge(carry, stats):
    top_old, den_old, num_old, acc_old, curv_old = carry
    top_new, den_new, num_new, acc_new, curv_new = stats
    top = jnp.maximum(top_old, top_new)
    keep_old = jnp.exp(top_old - top)
    keep_new = jnp.exp(top_new - top)
    return (top, keep_old * den_old + keep_new * den_new, keep_old[..., None] * num_old + keep_new[..., None] * num_new, keep_old[..., None] * acc_old + keep_new[..., None] * acc_new, keep_old * curv_old + keep_new * curv_new)

def finish(carry):
    top, den, num, acc, curv = carry
    attended = num / den[..., None]
    attended_tan = (acc - attended * curv[..., None]) / den[..., None]
    return (attended.astype(jnp.bfloat16), attended_tan.astype(jnp.bfloat16))

def head_pass(arrays):
    row_count = arrays[0].shape[0]
    level_count = (row_count // BLOCK).bit_length() - 1
    carry = leaf_terms(*arrays)
    current = arrays
    for level_num in range(1, level_count):
        current = tuple((pool_pairs(array) for array in current))
        carry = merge(carry, expand(pair_terms(current, level_num), 2 ** level_num))
    return finish(carry)

def reference(queries, keys, values, tan_queries, tan_keys, tan_values, w_out):
    row_count = queries.shape[0]

    def split_heads(array):
        return array.reshape(row_count, HEADS, HD).transpose(1, 0, 2)
    attended, attended_tan = lax.map(head_pass, tuple((split_heads(array) for array in (queries, keys, values, tan_queries, tan_keys, tan_values))))

    def join_heads(array):
        return array.transpose(1, 0, 2).reshape(row_count, HEADS * HD)
    stacked = jnp.concatenate([join_heads(attended), join_heads(attended_tan)], axis=0)
    group_cols = D // N_HEAD
    total = jnp.zeros((D, 2 * row_count), jnp.float32)
    for group_num in range(N_HEAD):
        lower = group_num * group_cols
        partial_term = jnp.dot(w_out[lower:lower + group_cols].T, stacked[:, lower:lower + group_cols].T, preferred_element_type=jnp.float32)
        total = total + lax.optimization_barrier(partial_term.astype(jnp.bfloat16)).astype(jnp.float32)
    result = total.astype(jnp.bfloat16)
    return (result[:, :row_count], result[:, row_count:])
```

```python
import math

import jax
import jax.numpy as jnp
from jax import lax
from jax.experimental import pallas as pl
from jax.experimental.pallas import tpu as pltpu
from jax.sharding import PartitionSpec as P

HD = 128
NX = 4
NZ = 8
NY = 4
HEADS_HERE = 4
LEAF = 256
MASKED = -1e30
LOG_TWO = math.log(2.0)
SCALE = 1.0 / math.sqrt(HD)
F32 = jnp.float32
BF16 = jnp.bfloat16
VMEM = pl.BlockSpec(memory_space=pltpu.VMEM)
SMEM = pl.BlockSpec(memory_space=pltpu.SMEM)
PARAMS = pltpu.CompilerParams(vmem_limit_bytes=40 * 1024 * 1024)


def dot(a, b):
    return lax.dot_general(a, b, (((1,), (0,)), ((), ())), preferred_element_type=F32)


def dot_nt(a, b):
    return lax.dot_general(a, b, (((1,), (1,)), ((), ())), preferred_element_type=F32)


def pool_matrix(rows):
    out = lax.broadcasted_iota(jnp.int32, (rows, 2 * rows), 0)
    src = lax.broadcasted_iota(jnp.int32, (rows, 2 * rows), 1)
    return jnp.where((src >> 1) == out, 0.5, 0.0).astype(BF16)


def pool(array):
    return dot(pool_matrix(array.shape[0] // 2), array).astype(BF16)


def attend(qq, kv, offset, mask=None):
    scores = dot_nt(qq[:, :HD], kv[:, HD : 2 * HD]) * SCALE + offset
    slopes = dot_nt(qq, kv[:, : 2 * HD]) * SCALE
    if mask is not None:
        scores = jnp.where(mask, scores, MASKED)
    top = jnp.max(scores, axis=1, keepdims=True)
    probs = jnp.exp(scores - top)
    moved = probs * slopes
    den = jnp.sum(probs, axis=1, keepdims=True)
    curv = jnp.sum(moved, axis=1, keepdims=True)
    both = dot(probs.astype(BF16), kv[:, 2 * HD : 4 * HD])
    acc = dot(moved.astype(BF16), kv[:, 2 * HD : 3 * HD]) + both[:, HD:]
    inv = 1.0 / den
    att = both[:, :HD] * inv
    curv = curv * inv
    tan = acc * inv - att * curv
    return att, tan, curv, top + jnp.log(den)


def merge(one, two):
    att1, tan1, curv1, lse1 = one
    att2, tan2, curv2, lse2 = two
    top = jnp.maximum(lse1, lse2)
    e1 = jnp.exp(lse1 - top)
    e2 = jnp.exp(lse2 - top)
    den = e1 + e2
    inv = 1.0 / den
    w1 = e1 * inv
    w2 = e2 * inv
    att = w1 * att1 + w2 * att2
    tan = w1 * tan1 + w2 * tan2 + (w1 * w2) * ((att1 - att2) * (curv1 - curv2))
    return att, tan, w1 * curv1 + w2 * curv2, top + jnp.log(den)


def wide(stats):
    att, tan, curv, lse = stats
    return att, tan, jnp.broadcast_to(curv, att.shape), jnp.broadcast_to(lse, att.shape)


def double(stats, scratch):
    rows = stats[0].shape[0]
    for num, part in enumerate(stats):
        scratch[num, pl.ds(0, rows, 2), :] = part
        scratch[num, pl.ds(1, rows, 2), :] = part
    return tuple(scratch[num, 0 : 2 * rows, :] for num in range(4))


def pool_kernel(place, q, tq, tk, k, v, tv, o0, o1, o2, o3):
    x = place[1]
    matrix = pool_matrix(128)
    for step, out in ((1, o1), (3, o3), (2, o2), (0, o0)):
        head = lax.rem(x + step, NX)
        cols = pl.ds(pl.multiple_of(head * HD, HD), HD)
        for num, ref in enumerate((q, tq, tk, k, v, tv)):
            out[:, num * HD : (num + 1) * HD] = dot(matrix, ref[:, cols]).astype(BF16)


def leaf_kernel(q, tq, tk, k, v, tv, att_out, tan_out, stat_out):
    row = lax.broadcasted_iota(jnp.int32, (LEAF, LEAF), 0)
    col = lax.broadcasted_iota(jnp.int32, (LEAF, LEAF), 1)
    lane = lax.broadcasted_iota(jnp.int32, (LEAF, HD), 1)
    for head in range(HEADS_HERE):
        cols = slice(head * HD, (head + 1) * HD)
        qq = jnp.concatenate([q[:, cols], tq[:, cols]], axis=1)
        kv = jnp.concatenate([tk[:, cols], k[:, cols], v[:, cols], tv[:, cols]], axis=1)
        att, tan, curv, lse = attend(qq, kv, 0.0, row >= col)
        att_out[head] = att
        tan_out[head] = tan
        stat_out[head] = jnp.where(lane == 0, lse, curv)


def upper_kernel(place, r0, r1, r2, r3, l1, l2, q3, q4, q5, k3, k4, k5):
    x = place[1]
    for step, ref in enumerate((r0, r1, r2, r3)):
        at = lax.rem(x + NX - step, NX)
        l1[pl.ds(pl.multiple_of(at * 128, 128), 128), :] = ref[...]
    level2 = pool(l1[...])
    l2[...] = level2
    level3 = pool(level2)
    q3[...] = level3[:, : 2 * HD]
    k3[...] = level3[:, 2 * HD :]
    level4 = pool(level3)
    q4[...] = level4[:, : 2 * HD]
    k4[...] = level4[:, 2 * HD :]
    level5 = pool(level4)
    q5[...] = level5[:, : 2 * HD]
    k5[...] = level5[:, 2 * HD :]


def near_kernel(l1, l2, att_out, tan_out, stat_out):
    lane = lax.broadcasted_iota(jnp.int32, (128, HD), 1)
    work = (
        (l1, 128, 0, LOG_TWO),
        (l1, 384, 256, LOG_TWO),
        (l2, 128, 0, 2 * LOG_TWO),
    )
    for num, (ref, mine, before, offset) in enumerate(work):
        att, tan, curv, lse = attend(
            ref[mine : mine + 128, : 2 * HD], ref[before : before + 128, 2 * HD :], offset
        )
        att_out[num] = att
        tan_out[num] = tan
        stat_out[num] = jnp.where(lane == 0, lse, curv)


def far_kernel(
    place, q3, q4, q5, g3, g4a, g4b, g5a, g5b, g5c, g5d, n_att, n_tan, n_stat,
    o0, o1, o2, o3, scratch, packed,
):
    x = place[1]
    z = place[0]

    def level(q, parts, number, bit):
        kv = parts[0][...] if len(parts) == 1 else jnp.concatenate([p[...] for p in parts], axis=0)
        att, tan, curv, lse = wide(attend(q[...], kv, number * LOG_TWO))
        seen = ((z >> bit) & 1) == 1
        return att, tan, curv, jnp.where(seen, lse, MASKED)

    def near(num):
        stat = n_stat[num]
        return wide((n_att[num], n_tan[num], stat[:, 1:2], stat[:, 0:1]))

    carry = level(q5, (g5a, g5b, g5c, g5d), 5, 2)
    carry = merge(level(q4, (g4a, g4b), 4, 1), double(carry, scratch))
    carry = merge(level(q3, (g3,), 3, 0), double(carry, scratch))
    first = double(carry, scratch)
    low = tuple(part[:128] for part in first)
    high = merge(near(2), tuple(part[128:] for part in first))
    lane = lax.broadcasted_iota(jnp.int32, (128, HD), 1)
    for half, stats in enumerate((low, high)):
        all_rows = double(stats, scratch)
        pieces = (
            tuple(part[:128] for part in all_rows),
            merge(near(half), tuple(part[128:] for part in all_rows)),
        )
        for num, (att, tan, curv, lse) in enumerate(pieces):
            rows = slice((2 * half + num) * 128, (2 * half + num + 1) * 128)
            packed[rows, 0:HD] = att.astype(BF16)
            packed[rows, HD : 2 * HD] = tan.astype(BF16)
            stat = jnp.zeros((128, HD), F32)
            at = 0
            for value in (lse, curv):
                for _ in range(3):
                    piece = value.astype(BF16).astype(F32)
                    stat = jnp.where(lane == at, piece, stat)
                    value = value - piece
                    at += 1
            packed[rows, 2 * HD : 3 * HD] = stat.astype(BF16)
    for step, out in enumerate((o0, o1, o2, o3)):
        to = lax.rem(x + step, NX)
        out[...] = packed[pl.ds(pl.multiple_of(to * 128, 128), 128), :]


def finish_kernel(place, b0, b1, b2, b3, l_att, l_tan, l_stat, out, scratch):
    x = place[1]
    for step, ref in enumerate((b0, b1, b2, b3)):
        head = lax.rem(x + NX - step, NX)
        stat = ref[:, 2 * HD : 3 * HD].astype(F32)
        lse = stat[:, 0:1] + stat[:, 1:2] + stat[:, 2:3]
        curv = stat[:, 3:4] + stat[:, 4:5] + stat[:, 5:6]
        rest = wide((ref[:, 0:HD].astype(F32), ref[:, HD : 2 * HD].astype(F32), curv, lse))
        rest = double(rest, scratch)
        mine = l_stat[head]
        leaf = wide((l_att[head], l_tan[head], mine[:, 1:2], mine[:, 0:1]))
        att, tan, _, _ = merge(leaf, rest)
        cols = pl.ds(pl.multiple_of(head * HD, HD), HD)
        out[0:LEAF, cols] = att.astype(BF16)
        out[LEAF : 2 * LEAF, cols] = tan.astype(BF16)


def weight_kernel(place, w_mine, w_other, mine, other):
    mine[0] = w_mine[...].T
    other[0] = w_other[...].T


def project(w1, w2, a1, a2):
    return dot_nt(w1, a1[...]) + dot_nt(w2, a2[...])


def far_chunk_kernel(w1, w2, a1, a2, half_a, half_b):
    both = project(w1[0], w2[0], a1, a2).astype(BF16)
    half_a[...] = both[:256]
    half_b[...] = both[256:]


def near_chunk_kernel(u1, u2, d1, d2, a1, a2, up_b, down_a):
    up_b[...] = project(u1[0, 256:], u2[0, 256:], a1, a2).astype(BF16)
    down_a[...] = project(d1[0, :256], d2[0, :256], a1, a2).astype(BF16)


def own_chunk_kernel(u1, u2, d1, d2, m1, m2, a1, a2, up_a, down_b, own):
    up_a[...] = project(u1[0, :256], u2[0, :256], a1, a2)
    down_b[...] = project(d1[0, 256:], d2[0, 256:], a1, a2)
    own[...] = project(m1[0], m2[0], a1, a2)


def relay_kernel(up_a, got_a, down_b, got_b, send_up, send_down):
    send_up[...] = (up_a[...] + got_a[...].astype(F32)).astype(BF16)
    send_down[...] = (down_b[...] + got_b[...].astype(F32)).astype(BF16)


def total_kernel(own, from_down_a, from_up_a, from_down_b, from_up_b, out, out_tan):
    top = own[:256] + from_down_a[...].astype(F32) + from_up_a[...].astype(F32)
    low = own[256:] + from_down_b[...].astype(F32) + from_up_b[...].astype(F32)
    out[0:256] = top[:, :256].astype(BF16)
    out[256:] = low[:, :256].astype(BF16)
    out_tan[0:256] = top[:, 256:].astype(BF16)
    out_tan[256:] = low[:, 256:].astype(BF16)


def shape(dims, kind=BF16):
    return jax.ShapeDtypeStruct(dims, kind)


def call(kernel, outs, specs, name, flops, size, scratch=(), out_specs=None, grid=()):
    return pl.pallas_call(
        kernel,
        out_shape=outs,
        in_specs=specs,
        out_specs=jax.tree.map(lambda _: VMEM, outs) if out_specs is None else out_specs,
        scratch_shapes=list(scratch),
        grid=grid,
        compiler_params=PARAMS,
        cost_estimate=pl.CostEstimate(flops=flops, bytes_accessed=size, transcendentals=0),
        name=name,
    )


def x_route(step):
    return [(z * NX + x, z * NX + (x + step) % NX) for z in range(NZ) for x in range(NX)]


def z_route(flip, bit):
    return [
        (z * NX + x, (z ^ flip) * NX + x)
        for z in range(NZ)
        if not (z >> bit) & 1
        for x in range(NX)
    ]


def y_route(step):
    return [(y * 2 + c, ((y + step) % NY) * 2 + c) for y in range(NY) for c in range(2)]


def core_route():
    return [(i, i ^ 1) for i in range(2 * NY)]


def after(first, *rest):
    return lax.optimization_barrier((first,) + rest)


def on_device(queries, keys, values, tan_queries, tan_keys, tan_values, w_out):
    ctx = lax.axis_index("ctx")
    head = lax.axis_index("head")
    place = jnp.stack([ctx // NX, ctx % NX, head // 2, head % 2]).astype(jnp.int32)
    packed_in = (queries, tan_queries, tan_keys, keys, values, tan_values)

    level1 = shape((128, 6 * HD))
    o0, o1, o2, o3 = call(
        pool_kernel, (level1,) * 4, [SMEM] + [VMEM] * 6, "pool", 10**9, 3 * 2**20
    )(place, *packed_in)
    r1 = lax.ppermute(o1, "ctx", x_route(1))
    r3 = lax.ppermute(o3, "ctx", x_route(3))
    r2 = lax.ppermute(o2, "ctx", x_route(2))

    _, *leaf_in = after(o1, *packed_in)
    leaf = call(
        leaf_kernel,
        (shape((4, LEAF, HD), F32),) * 3,
        [VMEM] * 6,
        "leaf",
        3 * 10**9,
        4 * 2**20,
    )(*leaf_in)
    _, w_later = after(o1, w_out)
    w_mine, w_other = pl.pallas_call(
        weight_kernel,
        out_shape=(shape((NY, 512, 512)),) * 2,
        grid_spec=pltpu.PrefetchScalarGridSpec(
            num_scalar_prefetch=1,
            grid=(NY,),
            in_specs=[
                pl.BlockSpec((512, 512), lambda j, p: (0, ((p[2] + j) % NY) * 2 + p[3])),
                pl.BlockSpec((512, 512), lambda j, p: (0, ((p[2] + j) % NY) * 2 + 1 - p[3])),
            ],
            out_specs=[pl.BlockSpec((1, 512, 512), lambda j, p: (j, 0, 0))] * 2,
        ),
        compiler_params=PARAMS,
        cost_estimate=pl.CostEstimate(flops=0, bytes_accessed=10 * 2**20, transcendentals=0),
        name="weights",
    )(place, w_later, w_later)
    w_pair = lax.ppermute(w_other, "head", core_route())

    l1, l2, q3, q4, q5, k3, k4, k5 = call(
        upper_kernel,
        (
            shape((512, 6 * HD)),
            shape((256, 6 * HD)),
            shape((128, 2 * HD)),
            shape((64, 2 * HD)),
            shape((32, 2 * HD)),
            shape((128, 4 * HD)),
            shape((64, 4 * HD)),
            shape((32, 4 * HD)),
        ),
        [SMEM] + [VMEM] * 4,
        "upper",
        10**9,
        3 * 2**20,
    )(place, o0, r1, r2, r3)
    g4 = [lax.ppermute(k4, "ctx", z_route(flip, 1)) for flip in (2, 3)]
    g5 = [lax.ppermute(k5, "ctx", z_route(flip, 2)) for flip in (4, 5, 6, 7)]
    g3 = lax.ppermute(k3, "ctx", z_route(1, 0))
    near = call(
        near_kernel,
        (shape((3, 128, HD), F32),) * 3,
        [VMEM] * 2,
        "near",
        10**9,
        2 * 2**20,
    )(l1, l2)
    back = shape((128, 3 * HD))
    s0, s1, s2, s3 = call(
        far_kernel,
        (back,) * 4,
        [SMEM] + [VMEM] * 13,
        "far",
        10**9,
        2 * 2**20,
        scratch=[pltpu.VMEM((4, 256, HD), F32), pltpu.VMEM((512, 3 * HD), BF16)],
    )(place, q3, q4, q5, g3, *g4, *g5, *near)
    b1 = lax.ppermute(s1, "ctx", x_route(1))
    b3 = lax.ppermute(s3, "ctx", x_route(3))
    b2 = lax.ppermute(s2, "ctx", x_route(2))

    rows = 2 * LEAF
    mine = call(
        finish_kernel,
        shape((rows, 4 * HD)),
        [SMEM] + [VMEM] * 7,
        "finish",
        10**8,
        3 * 2**20,
        scratch=[pltpu.VMEM((4, 256, HD), F32)],
    )(place, s0, b1, b2, b3, *leaf)
    pair = lax.ppermute(mine, "head", core_route())

    def chunk(j):
        return pl.BlockSpec((1, 512, 512), lambda i, j=j: (j, 0, 0))

    whole = pl.BlockSpec((rows, 4 * HD), lambda i: (0, 0))
    half = pl.BlockSpec((256, rows), lambda i: (0, 0))
    full = pl.BlockSpec((512, rows), lambda i: (0, 0))
    far_a, far_b = call(
        far_chunk_kernel,
        (shape((256, rows)),) * 2,
        [chunk(2)] * 2 + [whole] * 2,
        "chunk_far",
        5 * 10**8,
        2 * 2**20,
        out_specs=(half,) * 2,
        grid=(1,),
    )(w_mine, w_pair, mine, pair)
    got_a = lax.ppermute(far_a, "head", y_route(1))
    got_b = lax.ppermute(far_b, "head", y_route(3))
    _, mine2, pair2 = after(far_a, mine, pair)
    up_b, down_a = call(
        near_chunk_kernel,
        (shape((256, rows)),) * 2,
        [chunk(1)] * 2 + [chunk(3)] * 2 + [whole] * 2,
        "chunk_near",
        5 * 10**8,
        3 * 2**20,
        out_specs=(half,) * 2,
        grid=(1,),
    )(w_mine, w_pair, w_mine, w_pair, mine2, pair2)
    from_down_b = lax.ppermute(up_b, "head", y_route(1))
    from_up_a = lax.ppermute(down_a, "head", y_route(3))
    _, mine3, pair3 = after(up_b, mine, pair)
    up_a, down_b, own = call(
        own_chunk_kernel,
        (shape((256, rows), F32),) * 2 + (shape((512, rows), F32),),
        [chunk(1)] * 2 + [chunk(3)] * 2 + [chunk(0)] * 2 + [whole] * 2,
        "chunk_own",
        10**9,
        5 * 2**20,
        out_specs=(half, half, full),
        grid=(1,),
    )(w_mine, w_pair, w_mine, w_pair, w_mine, w_pair, mine3, pair3)
    send_up, send_down = call(
        relay_kernel, (shape((256, rows)),) * 2, [VMEM] * 4, "relay", 10**6, 2 * 2**20
    )(up_a, got_a, down_b, got_b)
    from_down_a = lax.ppermute(send_up, "head", y_route(1))
    from_up_b = lax.ppermute(send_down, "head", y_route(3))
    return call(
        total_kernel,
        (shape((512, LEAF)),) * 2,
        [VMEM] * 5,
        "total",
        10**6,
        3 * 2**20,
    )(own, from_down_a, from_up_a, from_down_b, from_up_b)


def solution(mesh):
    return jax.shard_map(
        on_device,
        mesh=mesh,
        in_specs=(P("ctx", "head"),) * 6 + (P("head", None),),
        out_specs=(P("head", "ctx"), P("head", "ctx")),
        check_vma=False,
    )
```

```python
import math

import jax
import jax.numpy as jnp
from jax import lax
from jax.experimental import pallas as pl
from jax.experimental.pallas import tpu as pltpu
from jax.sharding import PartitionSpec as P

HD = 128
NX = 4
NZ = 8
NY = 4
HEADS_HERE = 4
LEAF = 256
MASKED = -1e30
LOG_TWO = math.log(2.0)
SCALE = 1.0 / math.sqrt(HD)
F32 = jnp.float32
BF16 = jnp.bfloat16
VMEM = pl.BlockSpec(memory_space=pltpu.VMEM)
HBM = pl.BlockSpec(memory_space=pltpu.HBM)
PARAMS = pltpu.CompilerParams(vmem_limit_bytes=40 * 1024 * 1024)
LARGE = pltpu.CompilerParams(vmem_limit_bytes=62400000)


def dot(a, b):
    return lax.dot_general(a, b, (((1,), (0,)), ((), ())), preferred_element_type=F32)


def dot_nt(a, b):
    return lax.dot_general(a, b, (((1,), (1,)), ((), ())), preferred_element_type=F32)


def pool_matrix(rows):
    out = lax.broadcasted_iota(jnp.int32, (rows, 2 * rows), 0)
    src = lax.broadcasted_iota(jnp.int32, (rows, 2 * rows), 1)
    return jnp.where((src >> 1) == out, 0.5, 0.0).astype(BF16)


def pool(array):
    return dot(pool_matrix(array.shape[0] // 2), array).astype(BF16)


def attend(qq, kv, offset, mask=None):
    scores = dot_nt(qq[:, :HD], kv[:, HD : 2 * HD]) * SCALE + offset
    slopes = dot_nt(qq, kv[:, : 2 * HD]) * SCALE
    if mask is not None:
        scores = jnp.where(mask, scores, MASKED)
    top = jnp.max(scores, axis=1, keepdims=True)
    probs = jnp.exp(scores - top)
    moved = probs * slopes
    den = jnp.sum(probs, axis=1, keepdims=True)
    curv = jnp.sum(moved, axis=1, keepdims=True)
    both = dot(probs.astype(BF16), kv[:, 2 * HD : 4 * HD])
    acc = dot(moved.astype(BF16), kv[:, 2 * HD : 3 * HD]) + both[:, HD:]
    inv = 1.0 / den
    att = both[:, :HD] * inv
    curv = curv * inv
    tan = acc * inv - att * curv
    return att, tan, curv, top + jnp.log(den)


def merge(one, two):
    att1, tan1, curv1, lse1 = one
    att2, tan2, curv2, lse2 = two
    top = jnp.maximum(lse1, lse2)
    e1 = jnp.exp(lse1 - top)
    e2 = jnp.exp(lse2 - top)
    den = e1 + e2
    inv = 1.0 / den
    w1 = e1 * inv
    w2 = e2 * inv
    att = w1 * att1 + w2 * att2
    tan = w1 * tan1 + w2 * tan2 + (w1 * w2) * ((att1 - att2) * (curv1 - curv2))
    return att, tan, w1 * curv1 + w2 * curv2, top + jnp.log(den)


def wide(stats):
    att, tan, curv, lse = stats
    return att, tan, jnp.broadcast_to(curv, att.shape), jnp.broadcast_to(lse, att.shape)


def double(stats, scratch):
    rows = stats[0].shape[0]
    for num, part in enumerate(stats):
        scratch[num, pl.ds(0, rows, 2), :] = part
        scratch[num, pl.ds(1, rows, 2), :] = part
    return tuple(scratch[num, 0 : 2 * rows, :] for num in range(4))


def here():
    ctx = lax.axis_index("ctx")
    return lax.div(ctx, NX), lax.rem(ctx, NX)


def pool_kernel(tk, k, v, tv, q, tq, t0, t1, t2, t3, o0, o1, o2, o3, landed, keys1, sems):
    _, x = here()
    lanes = (2, 3, 4, 5, 0, 1)
    copies = [
        pltpu.make_async_copy(ref, landed.at[num], sems.at[num])
        for num, ref in enumerate((tk, k, v, tv, q, tq))
    ]
    for copy in copies:
        copy.start()
    matrix = pool_matrix(128)
    for num, copy in enumerate(copies):
        copy.wait()
        at = slice(lanes[num] * HD, (lanes[num] + 1) * HD)
        for step, out in enumerate((o0, o1, o2, o3)):
            head = lax.rem(x + step, NX)
            cols = pl.ds(pl.multiple_of(head * HD, HD), HD)
            rows = dot(matrix, landed[num, :, cols]).astype(BF16)
            out[:, at] = rows
            if num < 4:
                low = (step * 4 + num) * HD
                keys1[:, low : low + HD] = rows
    keys3 = pool(pool(keys1[...]))
    for step, out in enumerate((t0, t1, t2, t3)):
        out[...] = keys3[:, step * 4 * HD : (step + 1) * 4 * HD]


def top_kernel(t0, t1, t2, t3, k3, k4, k5):
    keys3 = jnp.concatenate([t0[...], t1[...], t2[...], t3[...]], axis=0)
    k3[...] = keys3
    keys4 = pool(keys3)
    k4[...] = keys4
    k5[...] = pool(keys4)


def mix_kernel(k3, k4, g4, one, two):
    one[0:128, :] = k3[...]
    one[128:160, :] = g4[...]
    two[0:64, :] = k4[...]
    two[64:96, :] = g4[...]


def leaf_kernel(q, tq, tk, k, v, tv, att_out, tan_out, stat_out, landed, sems):
    copies = [
        pltpu.make_async_copy(ref, landed.at[num], sems.at[num])
        for num, ref in enumerate((q, tq, tk, k, v, tv))
    ]
    for copy in copies:
        copy.start()
    for copy in copies:
        copy.wait()
    row = lax.broadcasted_iota(jnp.int32, (LEAF, LEAF), 0)
    col = lax.broadcasted_iota(jnp.int32, (LEAF, LEAF), 1)
    lane = lax.broadcasted_iota(jnp.int32, (LEAF, HD), 1)
    for head in range(HEADS_HERE):
        cols = slice(head * HD, (head + 1) * HD)
        qq = jnp.concatenate([landed[num, :, cols] for num in (0, 1)], axis=1)
        kv = jnp.concatenate([landed[num, :, cols] for num in (2, 3, 4, 5)], axis=1)
        att, tan, curv, lse = attend(qq, kv, 0.0, row >= col)
        att_out[head] = att
        tan_out[head] = tan
        stat_out[head] = jnp.where(lane == 0, lse, curv)


def upper_kernel(r0, r1, r2, r3, l1, l2, q3, q4, q5):
    _, x = here()
    for step, ref in enumerate((r0, r1, r2, r3)):
        at = lax.rem(x + NX - step, NX)
        l1[pl.ds(pl.multiple_of(at * 128, 128), 128), :] = ref[...]
    level2 = pool(l1[...])
    l2[...] = level2
    level3 = pool(level2[:, : 2 * HD])
    q3[...] = level3
    level4 = pool(level3)
    q4[...] = level4
    q5[...] = pool(level4)


def near_kernel(l1, l2, att_out, tan_out, stat_out):
    lane = lax.broadcasted_iota(jnp.int32, (128, HD), 1)
    work = (
        (l1, 128, 0, LOG_TWO),
        (l1, 384, 256, LOG_TWO),
        (l2, 128, 0, 2 * LOG_TWO),
    )
    for num, (ref, mine, before, offset) in enumerate(work):
        att, tan, curv, lse = attend(
            ref[mine : mine + 128, : 2 * HD], ref[before : before + 128, 2 * HD :], offset
        )
        att_out[num] = att
        tan_out[num] = tan
        stat_out[num] = jnp.where(lane == 0, lse, curv)


def far_kernel(
    q3, q4, q5, g4, g1, g2, g3, n_att, n_tan, n_stat, o0, o1, o2, o3, scratch, packed
):
    z, x = here()

    def level(q, keys, number, bit):
        att, tan, curv, lse = wide(attend(q[...], keys, number * LOG_TWO))
        seen = ((z >> bit) & 1) == 1
        return att, tan, curv, jnp.where(seen, lse, MASKED)

    def near(num):
        stat = n_stat[num]
        return wide((n_att[num], n_tan[num], stat[:, 1:2], stat[:, 0:1]))

    keys5 = jnp.concatenate([g4[...], g1[128:160, :], g2[64:96, :], g3[64:96, :]], axis=0)
    carry = level(q5, keys5, 5, 2)
    keys4 = jnp.concatenate([g2[0:64, :], g3[0:64, :]], axis=0)
    carry = merge(level(q4, keys4, 4, 1), double(carry, scratch))
    carry = merge(level(q3, g1[0:128, :], 3, 0), double(carry, scratch))
    first = double(carry, scratch)
    low = tuple(part[:128] for part in first)
    high = merge(near(2), tuple(part[128:] for part in first))
    lane = lax.broadcasted_iota(jnp.int32, (128, HD), 1)
    for half, stats in enumerate((low, high)):
        all_rows = double(stats, scratch)
        pieces = (
            tuple(part[:128] for part in all_rows),
            merge(near(half), tuple(part[128:] for part in all_rows)),
        )
        for num, (att, tan, curv, lse) in enumerate(pieces):
            rows = slice((2 * half + num) * 128, (2 * half + num + 1) * 128)
            packed[rows, 0:HD] = att.astype(BF16)
            packed[rows, HD : 2 * HD] = tan.astype(BF16)
            stat = jnp.zeros((128, HD), F32)
            at = 0
            for value in (lse, curv):
                for _ in range(3):
                    piece = value.astype(BF16).astype(F32)
                    stat = jnp.where(lane == at, piece, stat)
                    value = value - piece
                    at += 1
            packed[rows, 2 * HD : 3 * HD] = stat.astype(BF16)
    for step, out in enumerate((o0, o1, o2, o3)):
        to = lax.rem(x + step, NX)
        out[...] = packed[pl.ds(pl.multiple_of(to * 128, 128), 128), :]


def finish_kernel(b0, b1, b2, b3, l_att, l_tan, l_stat, out, scratch):
    _, x = here()
    for step, ref in enumerate((b0, b1, b2, b3)):
        head = lax.rem(x + NX - step, NX)
        stat = ref[:, 2 * HD : 3 * HD].astype(F32)
        lse = stat[:, 0:1] + stat[:, 1:2] + stat[:, 2:3]
        curv = stat[:, 3:4] + stat[:, 4:5] + stat[:, 5:6]
        rest = wide((ref[:, 0:HD].astype(F32), ref[:, HD : 2 * HD].astype(F32), curv, lse))
        rest = double(rest, scratch)
        mine = l_stat[head]
        leaf = wide((l_att[head], l_tan[head], mine[:, 1:2], mine[:, 0:1]))
        att, tan, _, _ = merge(leaf, rest)
        cols = pl.ds(pl.multiple_of(head * HD, HD), HD)
        out[0:LEAF, cols] = att.astype(BF16)
        out[LEAF : 2 * LEAF, cols] = tan.astype(BF16)


def weight_kernel(w, mine, other, landed, sems):
    head = lax.axis_index("head")
    y, core = lax.div(head, 2), lax.rem(head, 2)

    def block(step, flip):
        at = lax.rem(y + step, NY) * 2 + (1 - core if flip else core)
        return w.at[:, pl.ds(pl.multiple_of(at * 512, 512), 512)]

    work = [(step, flip) for flip in (1, 0) for step in range(NY)]
    copies = [
        pltpu.make_async_copy(block(step, flip), landed.at[num], sems.at[num])
        for num, (step, flip) in enumerate(work)
    ]
    for copy in copies:
        copy.start()
    for num, (step, flip) in enumerate(work):
        copies[num].wait()
        (other if flip else mine)[step] = landed[num].T


def project(w1, w2, a1, a2):
    return dot_nt(w1, a1[...]) + dot_nt(w2, a2[...])


def far_chunk_kernel(w1, w2, a1, a2, half_a, half_b):
    both = project(w1[0], w2[0], a1, a2).astype(BF16)
    half_a[...] = both[:256]
    half_b[...] = both[256:]


def near_chunk_kernel(u1, u2, d1, d2, a1, a2, up_b, down_a):
    up_b[...] = project(u1[0, 256:], u2[0, 256:], a1, a2).astype(BF16)
    down_a[...] = project(d1[0, :256], d2[0, :256], a1, a2).astype(BF16)


def own_chunk_kernel(u1, u2, d1, d2, m1, m2, a1, a2, up_a, down_b, own):
    up_a[...] = project(u1[0, :256], u2[0, :256], a1, a2)
    down_b[...] = project(d1[0, 256:], d2[0, 256:], a1, a2)
    own[...] = project(m1[0], m2[0], a1, a2)


def relay_kernel(up_a, got_a, down_b, got_b, send_up, send_down):
    send_up[...] = (up_a[...] + got_a[...].astype(F32)).astype(BF16)
    send_down[...] = (down_b[...] + got_b[...].astype(F32)).astype(BF16)


def total_kernel(own, from_down_a, from_up_a, from_down_b, from_up_b, out, out_tan):
    top = own[:256] + from_down_a[...].astype(F32) + from_up_a[...].astype(F32)
    low = own[256:] + from_down_b[...].astype(F32) + from_up_b[...].astype(F32)
    out[0:256] = top[:, :256].astype(BF16)
    out[256:] = low[:, :256].astype(BF16)
    out_tan[0:256] = top[:, 256:].astype(BF16)
    out_tan[256:] = low[:, 256:].astype(BF16)


def shape(dims, kind=BF16):
    return jax.ShapeDtypeStruct(dims, kind)


def call(kernel, outs, specs, name, flops, size, scratch=(), out_specs=None, grid=(), params=PARAMS):
    return pl.pallas_call(
        kernel,
        out_shape=outs,
        in_specs=specs,
        out_specs=jax.tree.map(lambda _: VMEM, outs) if out_specs is None else out_specs,
        scratch_shapes=list(scratch),
        grid=grid,
        compiler_params=params,
        cost_estimate=pl.CostEstimate(flops=flops, bytes_accessed=size, transcendentals=0),
        name=name,
    )


def x_route(step):
    return [(z * NX + x, z * NX + (x + step) % NX) for z in range(NZ) for x in range(NX)]


def z_route(flip):
    return [(z * NX + x, (z ^ flip) * NX + x) for z in range(NZ) for x in range(NX)]


def y_route(step):
    return [(y * 2 + c, ((y + step) % NY) * 2 + c) for y in range(NY) for c in range(2)]


def core_route():
    return [(i, i ^ 1) for i in range(2 * NY)]


def after(first, *rest):
    return lax.optimization_barrier((first,) + rest)


def on_device(queries, keys, values, tan_queries, tan_keys, tan_values, w_out):
    packed_in = (queries, tan_queries, tan_keys, keys, values, tan_values)

    level1 = shape((128, 6 * HD))
    keys3 = shape((32, 4 * HD))
    t0, t1, t2, t3, o0, o1, o2, o3 = call(
        pool_kernel,
        (keys3,) * 4 + (level1,) * 4,
        [HBM] * 6,
        "pool",
        10**9,
        4 * 2**20,
        scratch=[
            pltpu.VMEM((6, LEAF, 4 * HD), BF16),
            pltpu.VMEM((128, 16 * HD), BF16),
            pltpu.SemaphoreType.DMA((6,)),
        ],
        params=LARGE,
    )(tan_keys, keys, values, tan_values, queries, tan_queries)
    t1 = lax.ppermute(t1, "ctx", x_route(1))
    t3 = lax.ppermute(t3, "ctx", x_route(3))
    t2 = lax.ppermute(t2, "ctx", x_route(2))
    _, *leaf_in = after(o1, *packed_in)
    leaf = call(
        leaf_kernel,
        (shape((4, LEAF, HD), F32),) * 3,
        [HBM] * 6,
        "leaf",
        2 * 10**9,
        5 * 2**20,
        scratch=[pltpu.VMEM((6, LEAF, 4 * HD), BF16), pltpu.SemaphoreType.DMA((6,))],
    )(*leaf_in)
    t0, *leaf = after(t0, *leaf)
    k3, k4, k5 = call(
        top_kernel,
        (shape((128, 4 * HD)), shape((64, 4 * HD)), shape((32, 4 * HD))),
        [VMEM] * 4,
        "top",
        10**8,
        2**20,
    )(t0, t1, t2, t3)

    _, w_later = after(k5, w_out)
    w_mine, w_other = call(
        weight_kernel,
        (shape((NY, 512, 512)),) * 2,
        [HBM],
        "weights",
        10**6,
        12 * 2**20,
        scratch=[pltpu.VMEM((2 * NY, 512, 512), BF16), pltpu.SemaphoreType.DMA((2 * NY,))],
    )(w_later)
    k3, w_other = after(k3, w_other)

    g4 = lax.ppermute(k5, "ctx", z_route(7))
    one, two = call(
        mix_kernel,
        (shape((160, 4 * HD)), shape((96, 4 * HD))),
        [VMEM] * 3,
        "mix",
        10**6,
        2**19,
    )(k3, k4, g4)
    g2 = lax.ppermute(two, "ctx", z_route(2))
    g3 = lax.ppermute(two, "ctx", z_route(3))
    g1 = lax.ppermute(one, "ctx", z_route(1))

    _, o1, o2, o3 = after(k5, o1, o2, o3)
    r1 = lax.ppermute(o1, "ctx", x_route(1))
    r3 = lax.ppermute(o3, "ctx", x_route(3))
    r2 = lax.ppermute(o2, "ctx", x_route(2))
    l1, l2, q3, q4, q5 = call(
        upper_kernel,
        (
            shape((512, 6 * HD)),
            shape((256, 6 * HD)),
            shape((128, 2 * HD)),
            shape((64, 2 * HD)),
            shape((32, 2 * HD)),
        ),
        [VMEM] * 4,
        "upper",
        5 * 10**8,
        2 * 2**20,
    )(o0, r1, r2, r3)
    near = call(
        near_kernel,
        (shape((3, 128, HD), F32),) * 3,
        [VMEM] * 2,
        "near",
        5 * 10**8,
        2 * 2**20,
    )(l1, l2)

    back = shape((128, 3 * HD))
    s0, s1, s2, s3 = call(
        far_kernel,
        (back,) * 4,
        [VMEM] * 10,
        "far",
        10**9,
        4 * 2**20,
        scratch=[
            pltpu.VMEM((4, 256, HD), F32),
            pltpu.VMEM((512, 3 * HD), BF16),
        ],
    )(q3, q4, q5, g4, g1, g2, g3, *near)
    _, w_other = after(s1, w_other)
    w_pair = lax.ppermute(w_other, "head", core_route())
    b1 = lax.ppermute(s1, "ctx", x_route(1))
    b3 = lax.ppermute(s3, "ctx", x_route(3))
    b2 = lax.ppermute(s2, "ctx", x_route(2))

    rows = 2 * LEAF
    mine = call(
        finish_kernel,
        shape((rows, 4 * HD)),
        [VMEM] * 7,
        "finish",
        10**8,
        3 * 2**20,
        scratch=[pltpu.VMEM((4, 256, HD), F32)],
    )(s0, b1, b2, b3, *leaf)
    pair = lax.ppermute(mine, "head", core_route())

    def chunk(j):
        return pl.BlockSpec((1, 512, 512), lambda i, j=j: (j, 0, 0))

    whole = pl.BlockSpec((rows, 4 * HD), lambda i: (0, 0))
    half = pl.BlockSpec((256, rows), lambda i: (0, 0))
    full = pl.BlockSpec((512, rows), lambda i: (0, 0))
    far_a, far_b = call(
        far_chunk_kernel,
        (shape((256, rows)),) * 2,
        [chunk(2)] * 2 + [whole] * 2,
        "chunk_far",
        5 * 10**8,
        2 * 2**20,
        out_specs=(half,) * 2,
        grid=(1,),
    )(w_mine, w_pair, mine, pair)
    got_a = lax.ppermute(far_a, "head", y_route(1))
    got_b = lax.ppermute(far_b, "head", y_route(3))
    _, mine2, pair2 = after(far_a, mine, pair)
    up_b, down_a = call(
        near_chunk_kernel,
        (shape((256, rows)),) * 2,
        [chunk(1)] * 2 + [chunk(3)] * 2 + [whole] * 2,
        "chunk_near",
        5 * 10**8,
        3 * 2**20,
        out_specs=(half,) * 2,
        grid=(1,),
    )(w_mine, w_pair, w_mine, w_pair, mine2, pair2)
    from_down_b = lax.ppermute(up_b, "head", y_route(1))
    from_up_a = lax.ppermute(down_a, "head", y_route(3))
    _, mine3, pair3 = after(up_b, mine, pair)
    up_a, down_b, own = call(
        own_chunk_kernel,
        (shape((256, rows), F32),) * 2 + (shape((512, rows), F32),),
        [chunk(1)] * 2 + [chunk(3)] * 2 + [chunk(0)] * 2 + [whole] * 2,
        "chunk_own",
        10**9,
        5 * 2**20,
        out_specs=(half, half, full),
        grid=(1,),
    )(w_mine, w_pair, w_mine, w_pair, w_mine, w_pair, mine3, pair3)
    send_up, send_down = call(
        relay_kernel, (shape((256, rows)),) * 2, [VMEM] * 4, "relay", 10**6, 2 * 2**20
    )(up_a, got_a, down_b, got_b)
    from_down_a = lax.ppermute(send_up, "head", y_route(1))
    from_up_b = lax.ppermute(send_down, "head", y_route(3))
    return call(
        total_kernel,
        (shape((512, LEAF)),) * 2,
        [VMEM] * 5,
        "total",
        10**6,
        3 * 2**20,
    )(own, from_down_a, from_up_a, from_down_b, from_up_b)


def solution(mesh):
    return jax.shard_map(
        on_device,
        mesh=mesh,
        in_specs=(P("ctx", "head"),) * 6 + (P("head", None),),
        out_specs=(P("head", "ctx"), P("head", "ctx")),
        check_vma=False,
    )
```

```python
import math

import jax
import jax.numpy as jnp
from jax import lax
from jax.experimental import pallas as pl
from jax.experimental.pallas import tpu as pltpu
from jax.sharding import PartitionSpec as P

HD = 128
NX = 4
NZ = 8
NY = 4
HEADS_HERE = 4
LEAF = 256
MASKED = -1e30
LOG_TWO = math.log(2.0)
SCALE = 1.0 / math.sqrt(HD)
F32 = jnp.float32
BF16 = jnp.bfloat16
VMEM = pl.BlockSpec(memory_space=pltpu.VMEM)
HBM = pl.BlockSpec(memory_space=pltpu.HBM)
PARAMS = pltpu.CompilerParams(vmem_limit_bytes=40 * 1024 * 1024)
LARGE = pltpu.CompilerParams(vmem_limit_bytes=63300000)


def dot(a, b):
    return lax.dot_general(a, b, (((1,), (0,)), ((), ())), preferred_element_type=F32)


def dot_nt(a, b):
    return lax.dot_general(a, b, (((1,), (1,)), ((), ())), preferred_element_type=F32)


def pool_matrix(rows):
    out = lax.broadcasted_iota(jnp.int32, (rows, 2 * rows), 0)
    src = lax.broadcasted_iota(jnp.int32, (rows, 2 * rows), 1)
    return jnp.where((src >> 1) == out, 0.5, 0.0).astype(BF16)


def pool(array):
    return dot(pool_matrix(array.shape[0] // 2), array).astype(BF16)


def attend(qq, kv, offset, mask=None):
    scores = dot_nt(qq[:, :HD], kv[:, HD : 2 * HD]) * SCALE + offset
    slopes = dot_nt(qq, kv[:, : 2 * HD]) * SCALE
    if mask is not None:
        scores = jnp.where(mask, scores, MASKED)
    top = jnp.max(scores, axis=1, keepdims=True)
    probs = jnp.exp(scores - top)
    moved = probs * slopes
    den = jnp.sum(probs, axis=1, keepdims=True)
    curv = jnp.sum(moved, axis=1, keepdims=True)
    both = dot(probs.astype(BF16), kv[:, 2 * HD : 4 * HD])
    acc = dot(moved.astype(BF16), kv[:, 2 * HD : 3 * HD]) + both[:, HD:]
    inv = 1.0 / den
    att = both[:, :HD] * inv
    curv = curv * inv
    tan = acc * inv - att * curv
    return att, tan, curv, top + jnp.log(den)


def merge(one, two):
    att1, tan1, curv1, lse1 = one
    att2, tan2, curv2, lse2 = two
    top = jnp.maximum(lse1, lse2)
    e1 = jnp.exp(lse1 - top)
    e2 = jnp.exp(lse2 - top)
    den = e1 + e2
    inv = 1.0 / den
    w1 = e1 * inv
    w2 = e2 * inv
    att = w1 * att1 + w2 * att2
    tan = w1 * tan1 + w2 * tan2 + (w1 * w2) * ((att1 - att2) * (curv1 - curv2))
    return att, tan, w1 * curv1 + w2 * curv2, top + jnp.log(den)


def wide(stats):
    att, tan, curv, lse = stats
    return att, tan, jnp.broadcast_to(curv, att.shape), jnp.broadcast_to(lse, att.shape)


def double(stats, scratch):
    rows = stats[0].shape[0]
    for num, part in enumerate(stats):
        scratch[num, pl.ds(0, rows, 2), :] = part
        scratch[num, pl.ds(1, rows, 2), :] = part
    return tuple(scratch[num, 0 : 2 * rows, :] for num in range(4))


def here():
    ctx = lax.axis_index("ctx")
    return lax.div(ctx, NX), lax.rem(ctx, NX)


def lift_kernel(q, tq, tk, k, v, tv, t0, t1, t2, t3, landed, level3, sems):
    _, x = here()
    copies = [
        pltpu.make_async_copy(ref, landed.at[num], sems.at[num])
        for num, ref in enumerate((q, tq, tk, k, v, tv))
    ]
    for copy in copies:
        copy.start()
    out = lax.broadcasted_iota(jnp.int32, (32, LEAF), 0)
    src = lax.broadcasted_iota(jnp.int32, (32, LEAF), 1)
    matrix = jnp.where((src >> 3) == out, 0.125, 0.0).astype(BF16)
    for num, copy in enumerate(copies):
        copy.wait()
        level3[num] = dot(matrix, landed[num]).astype(BF16)
        for step, out in enumerate((t0, t1, t2, t3)):
            head = lax.rem(x + step, NX)
            cols = pl.ds(pl.multiple_of(head * HD, HD), HD)
            out[:, num * HD : (num + 1) * HD] = level3[num, :, cols]


def pool_kernel(q, tq, tk, k, v, tv, q1, q2, k1, k2):
    matrix = pool_matrix(128)
    for refs, out in (((q, tq), q1), ((tk, k, v, tv), k1)):
        for num, ref in enumerate(refs):
            rows = dot(matrix, ref[...]).astype(BF16)
            for head in range(HEADS_HERE):
                lanes = (head * len(refs) + num) * HD
                out[:, lanes : lanes + HD] = rows[:, head * HD : (head + 1) * HD]
    q2[...] = pool(q1[...])
    k2[...] = pool(k1[...])


def top_kernel(t0, t1, t2, t3, q3, q4, q5, k3, k4, k5):
    level3 = jnp.concatenate([t0[...], t1[...], t2[...], t3[...]], axis=0)
    level4 = pool(level3)
    level5 = pool(level4)
    for rows, q, k in ((level3, q3, k3), (level4, q4, k4), (level5, q5, k5)):
        q[...] = rows[:, : 2 * HD]
        k[...] = rows[:, 2 * HD :]


def mix_kernel(k3, k4, g4, one, two):
    one[0:128, :] = k3[...]
    one[128:160, :] = g4[...]
    two[0:64, :] = k4[...]
    two[64:96, :] = g4[...]


def leaf_kernel(q, tq, tk, k, v, tv, att_out, tan_out, stat_out):
    row = lax.broadcasted_iota(jnp.int32, (LEAF, LEAF), 0)
    col = lax.broadcasted_iota(jnp.int32, (LEAF, LEAF), 1)
    lane = lax.broadcasted_iota(jnp.int32, (LEAF, HD), 1)
    for head in range(HEADS_HERE):
        cols = slice(head * HD, (head + 1) * HD)
        qq = jnp.concatenate([q[:, cols], tq[:, cols]], axis=1)
        kv = jnp.concatenate([tk[:, cols], k[:, cols], v[:, cols], tv[:, cols]], axis=1)
        att, tan, curv, lse = attend(qq, kv, 0.0, row >= col)
        att_out[head] = att
        tan_out[head] = tan
        stat_out[head] = jnp.where(lane == 0, lse, curv)


def far_kernel(q3, q4, q5, g4, g1, g2, g3, o0, o1, o2, o3, scratch):
    z, _ = here()

    def level(q, keys, number, bit):
        att, tan, curv, lse = wide(attend(q[...], keys, number * LOG_TWO))
        seen = ((z >> bit) & 1) == 1
        return att, tan, curv, jnp.where(seen, lse, MASKED)

    keys5 = jnp.concatenate([g4[...], g1[128:160, :], g2[64:96, :], g3[64:96, :]], axis=0)
    carry = level(q5, keys5, 5, 2)
    keys4 = jnp.concatenate([g2[0:64, :], g3[0:64, :]], axis=0)
    carry = merge(level(q4, keys4, 4, 1), double(carry, scratch))
    carry = merge(level(q3, g1[0:128, :], 3, 0), double(carry, scratch))
    att, tan, curv, lse = carry
    lane = lax.broadcasted_iota(jnp.int32, (128, HD), 1)
    stat = jnp.zeros((128, HD), F32)
    at = 0
    for value in (lse, curv):
        for _ in range(3):
            piece = value.astype(BF16).astype(F32)
            stat = jnp.where(lane == at, piece, stat)
            value = value - piece
            at += 1
    for block, out in enumerate((o0, o3, o2, o1)):
        rows = slice(block * 32, (block + 1) * 32)
        out[:, 0:HD] = att[rows].astype(BF16)
        out[:, HD : 2 * HD] = tan[rows].astype(BF16)
        out[:, 2 * HD : 3 * HD] = stat[rows].astype(BF16)


def home_kernel(
    q1, q2, c1, c2, c3, l_att, l_tan, l_stat, att_out, tan_out, stat_out, scratch
):
    _, x = here()
    lane = lax.broadcasted_iota(jnp.int32, (LEAF, HD), 1)

    def level(queries, keys, number, bit):
        att, tan, curv, lse = wide(attend(queries, keys, number * LOG_TWO))
        seen = ((x >> bit) & 1) == 1
        return att, tan, curv, jnp.where(seen, lse, MASKED)

    for head in range(HEADS_HERE):
        qs = slice(head * 2 * HD, (head + 1) * 2 * HD)
        ks = slice(head * 4 * HD, (head + 1) * 4 * HD)
        keys2 = jnp.concatenate([c2[:, ks], c3[:, ks]], axis=0)
        carry = double(level(q2[:, qs], keys2, 2, 1), scratch)
        carry = double(merge(level(q1[:, qs], c1[:, ks], 1, 0), carry), scratch)
        mine = l_stat[head]
        leaf = wide((l_att[head], l_tan[head], mine[:, 1:2], mine[:, 0:1]))
        att, tan, curv, lse = merge(leaf, carry)
        att_out[head] = att
        tan_out[head] = tan
        stat_out[head] = jnp.where(lane == 0, lse, curv)


def finish_kernel(b0, b1, b2, b3, l_att, l_tan, l_stat, out, scratch):
    _, x = here()
    for step, ref in enumerate((b0, b1, b2, b3)):
        head = lax.rem(x + NX - step, NX)
        stat = ref[:, 2 * HD : 3 * HD].astype(F32)
        lse = stat[:, 0:1] + stat[:, 1:2] + stat[:, 2:3]
        curv = stat[:, 3:4] + stat[:, 4:5] + stat[:, 5:6]
        rest = wide((ref[:, 0:HD].astype(F32), ref[:, HD : 2 * HD].astype(F32), curv, lse))
        for _ in range(3):
            rest = double(rest, scratch)
        mine = l_stat[head]
        leaf = wide((l_att[head], l_tan[head], mine[:, 1:2], mine[:, 0:1]))
        att, tan, _, _ = merge(leaf, rest)
        cols = pl.ds(pl.multiple_of(head * HD, HD), HD)
        out[0:LEAF, cols] = att.astype(BF16)
        out[LEAF : 2 * LEAF, cols] = tan.astype(BF16)


def weight_kernel(w, mine, other, landed, sems):
    head = lax.axis_index("head")
    y, core = lax.div(head, 2), lax.rem(head, 2)

    def block(step, flip):
        at = lax.rem(y + step, NY) * 2 + (1 - core if flip else core)
        return w.at[:, pl.ds(pl.multiple_of(at * 512, 512), 512)]

    work = [(step, flip) for flip in (1, 0) for step in range(NY)]
    copies = [
        pltpu.make_async_copy(block(step, flip), landed.at[num], sems.at[num])
        for num, (step, flip) in enumerate(work)
    ]
    for copy in copies:
        copy.start()
    for num, (step, flip) in enumerate(work):
        copies[num].wait()
        (other if flip else mine)[step] = landed[num].T


def project(w1, w2, a1, a2):
    return dot_nt(w1, a1[...]) + dot_nt(w2, a2[...])


def far_chunk_kernel(w1, w2, a1, a2, half_a, half_b):
    both = project(w1[0], w2[0], a1, a2).astype(BF16)
    half_a[...] = both[:256]
    half_b[...] = both[256:]


def near_chunk_kernel(u1, u2, d1, d2, a1, a2, up_b, down_a):
    up_b[...] = project(u1[0, 256:], u2[0, 256:], a1, a2).astype(BF16)
    down_a[...] = project(d1[0, :256], d2[0, :256], a1, a2).astype(BF16)


def own_chunk_kernel(u1, u2, d1, d2, m1, m2, a1, a2, up_a, down_b, own):
    up_a[...] = project(u1[0, :256], u2[0, :256], a1, a2)
    down_b[...] = project(d1[0, 256:], d2[0, 256:], a1, a2)
    own[...] = project(m1[0], m2[0], a1, a2)


def relay_kernel(up_a, got_a, down_b, got_b, send_up, send_down):
    send_up[...] = (up_a[...] + got_a[...].astype(F32)).astype(BF16)
    send_down[...] = (down_b[...] + got_b[...].astype(F32)).astype(BF16)


def total_kernel(own, from_down_a, from_up_a, from_down_b, from_up_b, out, out_tan):
    top = own[:256] + from_down_a[...].astype(F32) + from_up_a[...].astype(F32)
    low = own[256:] + from_down_b[...].astype(F32) + from_up_b[...].astype(F32)
    out[0:256] = top[:, :256].astype(BF16)
    out[256:] = low[:, :256].astype(BF16)
    out_tan[0:256] = top[:, 256:].astype(BF16)
    out_tan[256:] = low[:, 256:].astype(BF16)


def shape(dims, kind=BF16):
    return jax.ShapeDtypeStruct(dims, kind)


def call(kernel, outs, specs, name, flops, size, scratch=(), out_specs=None, grid=(), params=PARAMS):
    return pl.pallas_call(
        kernel,
        out_shape=outs,
        in_specs=specs,
        out_specs=jax.tree.map(lambda _: VMEM, outs) if out_specs is None else out_specs,
        scratch_shapes=list(scratch),
        grid=grid,
        compiler_params=params,
        cost_estimate=pl.CostEstimate(flops=flops, bytes_accessed=size, transcendentals=0),
        name=name,
    )


def x_route(step):
    return [(z * NX + x, z * NX + (x + step) % NX) for z in range(NZ) for x in range(NX)]


def x_to(targets):
    return [(z * NX + x, z * NX + targets[x]) for z in range(NZ) for x in range(NX)]


def z_route(flip):
    return [(z * NX + x, (z ^ flip) * NX + x) for z in range(NZ) for x in range(NX)]


def y_route(step):
    return [(y * 2 + c, ((y + step) % NY) * 2 + c) for y in range(NY) for c in range(2)]


def core_route():
    return [(i, i ^ 1) for i in range(2 * NY)]


def after(first, *rest):
    return lax.optimization_barrier((first,) + rest)


def on_device(queries, keys, values, tan_queries, tan_keys, tan_values, w_out):
    packed_in = (queries, tan_queries, tan_keys, keys, values, tan_values)

    level3 = shape((32, 6 * HD))
    t0, t1, t2, t3 = call(
        lift_kernel,
        (level3,) * 4,
        [HBM] * 6,
        "lift",
        10**9,
        2 * 2**20,
        scratch=[
            pltpu.VMEM((6, LEAF, 4 * HD), BF16),
            pltpu.VMEM((6, 32, 4 * HD), BF16),
            pltpu.SemaphoreType.DMA((6,)),
        ],
        params=LARGE,
    )(*packed_in)
    o_lift = t1
    _, *pool_in = after(t1, *packed_in)
    q1, q2, k1, k2 = call(
        pool_kernel,
        (
            shape((128, 8 * HD)),
            shape((64, 8 * HD)),
            shape((128, 16 * HD)),
            shape((64, 16 * HD)),
        ),
        [VMEM] * 6,
        "pool",
        10**9,
        3 * 2**20,
    )(*pool_in)
    t1 = lax.ppermute(t1, "ctx", x_route(1))
    t3 = lax.ppermute(t3, "ctx", x_route(3))
    t2 = lax.ppermute(t2, "ctx", x_route(2))

    _, *leaf_in = after(o_lift, *packed_in)
    leaf = call(
        leaf_kernel,
        (shape((4, LEAF, HD), F32),) * 3,
        [VMEM] * 6,
        "leaf",
        2 * 10**9,
        5 * 2**20,
    )(*leaf_in)
    t0, *leaf = after(t0, *leaf)
    _, w_later = after(o_lift, w_out)
    w_mine, w_other = call(
        weight_kernel,
        (shape((NY, 512, 512)),) * 2,
        [HBM],
        "weights",
        10**6,
        12 * 2**20,
        scratch=[pltpu.VMEM((2 * NY, 512, 512), BF16), pltpu.SemaphoreType.DMA((2 * NY,))],
    )(w_later)
    t0, w_other = after(t0, w_other)

    t0, q1 = after(t0, q1)
    q3, q4, q5, k3, k4, k5 = call(
        top_kernel,
        tuple(shape((rows, lanes * HD)) for lanes in (2, 4) for rows in (128, 64, 32)),
        [VMEM] * 4,
        "top",
        10**8,
        2**20,
    )(t0, t1, t2, t3)

    g4 = lax.ppermute(k5, "ctx", z_route(7))

    _, k1, k2 = after(k5, k1, k2)
    c1 = lax.ppermute(k1, "ctx", x_to((1, 0, 3, 2)))
    c2 = lax.ppermute(k2, "ctx", x_to((2, 3, 1, 0)))
    c3 = lax.ppermute(k2, "ctx", x_to((3, 2, 1, 0)))

    one, two = call(
        mix_kernel,
        (shape((160, 4 * HD)), shape((96, 4 * HD))),
        [VMEM] * 3,
        "mix",
        10**6,
        2**19,
    )(k3, k4, g4)
    g2 = lax.ppermute(two, "ctx", z_route(2))
    g3 = lax.ppermute(two, "ctx", z_route(3))
    g1 = lax.ppermute(one, "ctx", z_route(1))

    q3, c1, c2, c3 = after(q3, c1, c2, c3)
    back = shape((32, 3 * HD))
    s0, s1, s2, s3 = call(
        far_kernel,
        (back,) * 4,
        [VMEM] * 7,
        "far",
        10**9,
        4 * 2**20,
        scratch=[pltpu.VMEM((4, 128, HD), F32)],
    )(q3, q4, q5, g4, g1, g2, g3)
    _, w_other = after(s1, w_other)
    w_pair = lax.ppermute(w_other, "head", core_route())
    b1 = lax.ppermute(s1, "ctx", x_route(1))
    b3 = lax.ppermute(s3, "ctx", x_route(3))
    b2 = lax.ppermute(s2, "ctx", x_route(2))

    _, q1, *leaf = after(s1, q1, *leaf)
    leaf = call(
        home_kernel,
        (shape((4, LEAF, HD), F32),) * 3,
        [VMEM] * 8,
        "home",
        2 * 10**9,
        4 * 2**20,
        scratch=[pltpu.VMEM((4, 256, HD), F32)],
    )(q1, q2, c1, c2, c3, *leaf)

    rows = 2 * LEAF
    mine = call(
        finish_kernel,
        shape((rows, 4 * HD)),
        [VMEM] * 7,
        "finish",
        10**8,
        3 * 2**20,
        scratch=[pltpu.VMEM((4, 256, HD), F32)],
    )(s0, b1, b2, b3, *leaf)
    pair = lax.ppermute(mine, "head", core_route())

    def chunk(j):
        return pl.BlockSpec((1, 512, 512), lambda i, j=j: (j, 0, 0))

    whole = pl.BlockSpec((rows, 4 * HD), lambda i: (0, 0))
    half = pl.BlockSpec((256, rows), lambda i: (0, 0))
    full = pl.BlockSpec((512, rows), lambda i: (0, 0))
    far_a, far_b = call(
        far_chunk_kernel,
        (shape((256, rows)),) * 2,
        [chunk(2)] * 2 + [whole] * 2,
        "chunk_far",
        5 * 10**8,
        2 * 2**20,
        out_specs=(half,) * 2,
        grid=(1,),
    )(w_mine, w_pair, mine, pair)
    got_a = lax.ppermute(far_a, "head", y_route(1))
    got_b = lax.ppermute(far_b, "head", y_route(3))
    _, mine2, pair2 = after(far_a, mine, pair)
    up_b, down_a = call(
        near_chunk_kernel,
        (shape((256, rows)),) * 2,
        [chunk(1)] * 2 + [chunk(3)] * 2 + [whole] * 2,
        "chunk_near",
        5 * 10**8,
        3 * 2**20,
        out_specs=(half,) * 2,
        grid=(1,),
    )(w_mine, w_pair, w_mine, w_pair, mine2, pair2)
    from_down_b = lax.ppermute(up_b, "head", y_route(1))
    from_up_a = lax.ppermute(down_a, "head", y_route(3))
    _, mine3, pair3 = after(up_b, mine, pair)
    up_a, down_b, own = call(
        own_chunk_kernel,
        (shape((256, rows), F32),) * 2 + (shape((512, rows), F32),),
        [chunk(1)] * 2 + [chunk(3)] * 2 + [chunk(0)] * 2 + [whole] * 2,
        "chunk_own",
        10**9,
        5 * 2**20,
        out_specs=(half, half, full),
        grid=(1,),
    )(w_mine, w_pair, w_mine, w_pair, w_mine, w_pair, mine3, pair3)
    send_up, send_down = call(
        relay_kernel, (shape((256, rows)),) * 2, [VMEM] * 4, "relay", 10**6, 2 * 2**20
    )(up_a, got_a, down_b, got_b)
    from_down_a = lax.ppermute(send_up, "head", y_route(1))
    from_up_b = lax.ppermute(send_down, "head", y_route(3))
    return call(
        total_kernel,
        (shape((512, LEAF)),) * 2,
        [VMEM] * 5,
        "total",
        10**6,
        3 * 2**20,
    )(own, from_down_a, from_up_a, from_down_b, from_up_b)


def solution(mesh):
    return jax.shard_map(
        on_device,
        mesh=mesh,
        in_specs=(P("ctx", "head"),) * 6 + (P("head", None),),
        out_specs=(P("head", "ctx"), P("head", "ctx")),
        check_vma=False,
    )
```

```python
import math

import jax
import jax.numpy as jnp
from jax import lax
from jax.experimental import pallas as pl
from jax.experimental.pallas import tpu as pltpu
from jax.sharding import PartitionSpec as P

HD = 128
NX = 4
NZ = 8
NY = 4
HEADS_HERE = 4
LEAF = 256
MASKED = -1e30
LOG_TWO = math.log(2.0)
SCALE = 1.0 / math.sqrt(HD)
F32 = jnp.float32
BF16 = jnp.bfloat16
VMEM = pl.BlockSpec(memory_space=pltpu.VMEM)
HBM = pl.BlockSpec(memory_space=pltpu.HBM)
PARAMS = pltpu.CompilerParams(vmem_limit_bytes=40 * 1024 * 1024)
LARGE = pltpu.CompilerParams(vmem_limit_bytes=63300000)


def dot(a, b):
    return lax.dot_general(a, b, (((1,), (0,)), ((), ())), preferred_element_type=F32)


def dot_nt(a, b):
    return lax.dot_general(a, b, (((1,), (1,)), ((), ())), preferred_element_type=F32)


def pool_matrix(rows):
    out = lax.broadcasted_iota(jnp.int32, (rows, 2 * rows), 0)
    src = lax.broadcasted_iota(jnp.int32, (rows, 2 * rows), 1)
    return jnp.where((src >> 1) == out, 0.5, 0.0).astype(BF16)


def pool(array):
    return dot(pool_matrix(array.shape[0] // 2), array).astype(BF16)


def attend(qq, kv, offset, mask=None):
    scores = dot_nt(qq[:, :HD], kv[:, HD : 2 * HD]) * SCALE + offset
    slopes = dot_nt(qq, kv[:, : 2 * HD]) * SCALE
    if mask is not None:
        scores = jnp.where(mask, scores, MASKED)
    top = jnp.max(scores, axis=1, keepdims=True)
    probs = jnp.exp(scores - top)
    moved = probs * slopes
    den = jnp.sum(probs, axis=1, keepdims=True)
    curv = jnp.sum(moved, axis=1, keepdims=True)
    both = dot(probs.astype(BF16), kv[:, 2 * HD : 4 * HD])
    acc = dot(moved.astype(BF16), kv[:, 2 * HD : 3 * HD]) + both[:, HD:]
    inv = 1.0 / den
    att = both[:, :HD] * inv
    curv = curv * inv
    tan = acc * inv - att * curv
    return att, tan, curv, top + jnp.log(den)


def merge(one, two):
    att1, tan1, curv1, lse1 = one
    att2, tan2, curv2, lse2 = two
    top = jnp.maximum(lse1, lse2)
    e1 = jnp.exp(lse1 - top)
    e2 = jnp.exp(lse2 - top)
    den = e1 + e2
    inv = 1.0 / den
    w1 = e1 * inv
    w2 = e2 * inv
    att = w1 * att1 + w2 * att2
    tan = w1 * tan1 + w2 * tan2 + (w1 * w2) * ((att1 - att2) * (curv1 - curv2))
    return att, tan, w1 * curv1 + w2 * curv2, top + jnp.log(den)


def wide(stats):
    att, tan, curv, lse = stats
    return att, tan, jnp.broadcast_to(curv, att.shape), jnp.broadcast_to(lse, att.shape)


def double(stats, scratch):
    rows = stats[0].shape[0]
    for num, part in enumerate(stats):
        scratch[num, pl.ds(0, rows, 2), :] = part
        scratch[num, pl.ds(1, rows, 2), :] = part
    return tuple(scratch[num, 0 : 2 * rows, :] for num in range(4))


def here():
    ctx = lax.axis_index("ctx")
    return lax.div(ctx, NX), lax.rem(ctx, NX)


def lift_kernel(q, tq, tk, k, v, tv, t0, t1, t2, t3, landed, level3, sems):
    _, x = here()
    copies = [
        pltpu.make_async_copy(ref, landed.at[num], sems.at[num])
        for num, ref in enumerate((q, tq, tk, k, v, tv))
    ]
    for copy in copies:
        copy.start()
    out = lax.broadcasted_iota(jnp.int32, (32, LEAF), 0)
    src = lax.broadcasted_iota(jnp.int32, (32, LEAF), 1)
    matrix = jnp.where((src >> 3) == out, 0.125, 0.0).astype(BF16)
    for num, copy in enumerate(copies):
        copy.wait()
        level3[num] = dot(matrix, landed[num]).astype(BF16)
        for step, out in enumerate((t0, t1, t2, t3)):
            head = lax.rem(x + step, NX)
            cols = pl.ds(pl.multiple_of(head * HD, HD), HD)
            out[:, num * HD : (num + 1) * HD] = level3[num, :, cols]


def pool_kernel(q, tq, tk, k, v, tv, q1, q2, k1, k2):
    matrix = pool_matrix(128)
    for refs, out in (((q, tq), q1), ((tk, k, v, tv), k1)):
        for num, ref in enumerate(refs):
            rows = dot(matrix, ref[...]).astype(BF16)
            for head in range(HEADS_HERE):
                lanes = (head * len(refs) + num) * HD
                out[:, lanes : lanes + HD] = rows[:, head * HD : (head + 1) * HD]
    q2[...] = pool(q1[...])
    k2[...] = pool(k1[...])


def top_kernel(t0, t1, t2, t3, q3, q4, q5, k3, k4, k5):
    level3 = jnp.concatenate([t0[...], t1[...], t2[...], t3[...]], axis=0)
    level4 = pool(level3)
    level5 = pool(level4)
    for rows, q, k in ((level3, q3, k3), (level4, q4, k4), (level5, q5, k5)):
        q[...] = rows[:, : 2 * HD]
        k[...] = rows[:, 2 * HD :]


def mix_kernel(k3, k4, g4, one, two):
    one[0:128, :] = k3[...]
    one[128:160, :] = g4[...]
    two[0:64, :] = k4[...]
    two[64:96, :] = g4[...]


def leaf_kernel(q, tq, tk, k, v, tv, att_out, tan_out, stat_out):
    row = lax.broadcasted_iota(jnp.int32, (LEAF, LEAF), 0)
    col = lax.broadcasted_iota(jnp.int32, (LEAF, LEAF), 1)
    lane = lax.broadcasted_iota(jnp.int32, (LEAF, HD), 1)
    for head in range(HEADS_HERE):
        cols = slice(head * HD, (head + 1) * HD)
        qq = jnp.concatenate([q[:, cols], tq[:, cols]], axis=1)
        kv = jnp.concatenate([tk[:, cols], k[:, cols], v[:, cols], tv[:, cols]], axis=1)
        att, tan, curv, lse = attend(qq, kv, 0.0, row >= col)
        att_out[head] = att
        tan_out[head] = tan
        stat_out[head] = jnp.where(lane == 0, lse, curv)


def far_kernel(q3, q4, q5, g4, g1, g2, g3, o0, o1, o2, o3, scratch):
    z, _ = here()

    def level(q, keys, number, bit):
        att, tan, curv, lse = wide(attend(q[...], keys, number * LOG_TWO))
        seen = ((z >> bit) & 1) == 1
        return att, tan, curv, jnp.where(seen, lse, MASKED)

    keys5 = jnp.concatenate([g4[...], g1[128:160, :], g2[64:96, :], g3[64:96, :]], axis=0)
    carry = level(q5, keys5, 5, 2)
    keys4 = jnp.concatenate([g2[0:64, :], g3[0:64, :]], axis=0)
    carry = merge(level(q4, keys4, 4, 1), double(carry, scratch))
    carry = merge(level(q3, g1[0:128, :], 3, 0), double(carry, scratch))
    att, tan, curv, lse = carry
    lane = lax.broadcasted_iota(jnp.int32, (128, HD), 1)
    stat = jnp.zeros((128, HD), F32)
    at = 0
    for value in (lse, curv):
        for _ in range(3):
            piece = value.astype(BF16).astype(F32)
            stat = jnp.where(lane == at, piece, stat)
            value = value - piece
            at += 1
    for block, out in enumerate((o0, o3, o2, o1)):
        rows = slice(block * 32, (block + 1) * 32)
        out[:, 0:HD] = att[rows].astype(BF16)
        out[:, HD : 2 * HD] = tan[rows].astype(BF16)
        out[:, 2 * HD : 3 * HD] = stat[rows].astype(BF16)


def home_kernel(
    q1, q2, c1, c2, c3, l_att, l_tan, l_stat, att_out, tan_out, stat_out, scratch
):
    _, x = here()
    lane = lax.broadcasted_iota(jnp.int32, (LEAF, HD), 1)

    def level(queries, keys, number, bit):
        att, tan, curv, lse = wide(attend(queries, keys, number * LOG_TWO))
        seen = ((x >> bit) & 1) == 1
        return att, tan, curv, jnp.where(seen, lse, MASKED)

    for head in range(HEADS_HERE):
        qs = slice(head * 2 * HD, (head + 1) * 2 * HD)
        ks = slice(head * 4 * HD, (head + 1) * 4 * HD)
        keys2 = jnp.concatenate([c2[:, ks], c3[:, ks]], axis=0)
        carry = double(level(q2[:, qs], keys2, 2, 1), scratch)
        carry = double(merge(level(q1[:, qs], c1[:, ks], 1, 0), carry), scratch)
        mine = l_stat[head]
        leaf = wide((l_att[head], l_tan[head], mine[:, 1:2], mine[:, 0:1]))
        att, tan, curv, lse = merge(leaf, carry)
        att_out[head] = att
        tan_out[head] = tan
        stat_out[head] = jnp.where(lane == 0, lse, curv)


def finish_kernel(b0, b1, b2, b3, l_att, l_tan, l_stat, out, scratch):
    _, x = here()
    for step, ref in enumerate((b0, b1, b2, b3)):
        head = lax.rem(x + NX - step, NX)
        stat = ref[:, 2 * HD : 3 * HD].astype(F32)
        lse = stat[:, 0:1] + stat[:, 1:2] + stat[:, 2:3]
        curv = stat[:, 3:4] + stat[:, 4:5] + stat[:, 5:6]
        rest = wide((ref[:, 0:HD].astype(F32), ref[:, HD : 2 * HD].astype(F32), curv, lse))
        for _ in range(3):
            rest = double(rest, scratch)
        mine = l_stat[head]
        leaf = wide((l_att[head], l_tan[head], mine[:, 1:2], mine[:, 0:1]))
        att, tan, _, _ = merge(leaf, rest)
        cols = pl.ds(pl.multiple_of(head * HD, HD), HD)
        out[0:LEAF, cols] = att.astype(BF16)
        out[LEAF : 2 * LEAF, cols] = tan.astype(BF16)


def weight_kernel(w, mine, other, landed, sems):
    head = lax.axis_index("head")
    y, core = lax.div(head, 2), lax.rem(head, 2)

    def block(step, flip):
        at = lax.rem(y + step, NY) * 2 + (1 - core if flip else core)
        return w.at[:, pl.ds(pl.multiple_of(at * 512, 512), 512)]

    work = [(step, flip) for flip in (1, 0) for step in range(NY)]
    copies = [
        pltpu.make_async_copy(block(step, flip), landed.at[num], sems.at[num])
        for num, (step, flip) in enumerate(work)
    ]
    for copy in copies:
        copy.start()
    for num, (step, flip) in enumerate(work):
        copies[num].wait()
        (other if flip else mine)[step] = landed[num].T


def begin_kernel(w_mine, mine, part):
    for step in (2, 1, 3, 0):
        part[step] = dot_nt(w_mine[step], mine[...])


def far_chunk_kernel(w, part, pair, half_a, half_b):
    half_a[...] = (part[0, :256] + dot_nt(w[0, :256], pair[...])).astype(BF16)
    half_b[...] = (part[0, 256:] + dot_nt(w[0, 256:], pair[...])).astype(BF16)


def near_chunk_kernel(wu, wd, pu, pd, pair, up_b, down_a):
    up_b[...] = (pu[0, 256:] + dot_nt(wu[0, 256:], pair[...])).astype(BF16)
    down_a[...] = (pd[0, :256] + dot_nt(wd[0, :256], pair[...])).astype(BF16)


def own_chunk_kernel(wu, wd, wm, pu, pd, pm, pair, up_a, down_b, own):
    up_a[...] = pu[0, :256] + dot_nt(wu[0, :256], pair[...])
    down_b[...] = pd[0, 256:] + dot_nt(wd[0, 256:], pair[...])
    own[...] = pm[0] + dot_nt(wm[0], pair[...])


def relay_kernel(up_a, got_a, down_b, got_b, send_up, send_down):
    send_up[...] = (up_a[...] + got_a[...].astype(F32)).astype(BF16)
    send_down[...] = (down_b[...] + got_b[...].astype(F32)).astype(BF16)


def total_kernel(own, from_down_a, from_up_a, from_down_b, from_up_b, out, out_tan):
    top = own[:256] + from_down_a[...].astype(F32) + from_up_a[...].astype(F32)
    low = own[256:] + from_down_b[...].astype(F32) + from_up_b[...].astype(F32)
    out[0:256] = top[:, :256].astype(BF16)
    out[256:] = low[:, :256].astype(BF16)
    out_tan[0:256] = top[:, 256:].astype(BF16)
    out_tan[256:] = low[:, 256:].astype(BF16)


def shape(dims, kind=BF16):
    return jax.ShapeDtypeStruct(dims, kind)


def call(kernel, outs, specs, name, flops, size, scratch=(), out_specs=None, grid=(), params=PARAMS):
    return pl.pallas_call(
        kernel,
        out_shape=outs,
        in_specs=specs,
        out_specs=jax.tree.map(lambda _: VMEM, outs) if out_specs is None else out_specs,
        scratch_shapes=list(scratch),
        grid=grid,
        compiler_params=params,
        cost_estimate=pl.CostEstimate(flops=flops, bytes_accessed=size, transcendentals=0),
        name=name,
    )


def x_route(step):
    return [(z * NX + x, z * NX + (x + step) % NX) for z in range(NZ) for x in range(NX)]


def x_to(targets):
    return [(z * NX + x, z * NX + targets[x]) for z in range(NZ) for x in range(NX)]


def z_route(flip):
    return [(z * NX + x, (z ^ flip) * NX + x) for z in range(NZ) for x in range(NX)]


def y_route(step):
    return [(y * 2 + c, ((y + step) % NY) * 2 + c) for y in range(NY) for c in range(2)]


def core_route():
    return [(i, i ^ 1) for i in range(2 * NY)]


def after(first, *rest):
    return lax.optimization_barrier((first,) + rest)


def on_device(queries, keys, values, tan_queries, tan_keys, tan_values, w_out):
    packed_in = (queries, tan_queries, tan_keys, keys, values, tan_values)

    level3 = shape((32, 6 * HD))
    t0, t1, t2, t3 = call(
        lift_kernel,
        (level3,) * 4,
        [HBM] * 6,
        "lift",
        10**9,
        2 * 2**20,
        scratch=[
            pltpu.VMEM((6, LEAF, 4 * HD), BF16),
            pltpu.VMEM((6, 32, 4 * HD), BF16),
            pltpu.SemaphoreType.DMA((6,)),
        ],
        params=LARGE,
    )(*packed_in)
    o_lift = t1
    _, *pool_in = after(t1, *packed_in)
    q1, q2, k1, k2 = call(
        pool_kernel,
        (
            shape((128, 8 * HD)),
            shape((64, 8 * HD)),
            shape((128, 16 * HD)),
            shape((64, 16 * HD)),
        ),
        [VMEM] * 6,
        "pool",
        10**9,
        3 * 2**20,
    )(*pool_in)
    t1 = lax.ppermute(t1, "ctx", x_route(1))
    t3 = lax.ppermute(t3, "ctx", x_route(3))
    t2 = lax.ppermute(t2, "ctx", x_route(2))

    _, *leaf_in = after(o_lift, *packed_in)
    leaf = call(
        leaf_kernel,
        (shape((4, LEAF, HD), F32),) * 3,
        [VMEM] * 6,
        "leaf",
        2 * 10**9,
        5 * 2**20,
    )(*leaf_in)
    t0, *leaf = after(t0, *leaf)
    _, w_later = after(o_lift, w_out)
    w_mine, w_other = call(
        weight_kernel,
        (shape((NY, 512, 512)),) * 2,
        [HBM],
        "weights",
        10**6,
        12 * 2**20,
        scratch=[pltpu.VMEM((2 * NY, 512, 512), BF16), pltpu.SemaphoreType.DMA((2 * NY,))],
    )(w_later)
    t0, w_other = after(t0, w_other)

    t0, q1 = after(t0, q1)
    q3, q4, q5, k3, k4, k5 = call(
        top_kernel,
        tuple(shape((rows, lanes * HD)) for lanes in (2, 4) for rows in (128, 64, 32)),
        [VMEM] * 4,
        "top",
        10**8,
        2**20,
    )(t0, t1, t2, t3)

    g4 = lax.ppermute(k5, "ctx", z_route(7))

    _, k1, k2 = after(k5, k1, k2)
    c1 = lax.ppermute(k1, "ctx", x_to((1, 0, 3, 2)))
    c2 = lax.ppermute(k2, "ctx", x_to((2, 3, 1, 0)))
    c3 = lax.ppermute(k2, "ctx", x_to((3, 2, 1, 0)))

    one, two = call(
        mix_kernel,
        (shape((160, 4 * HD)), shape((96, 4 * HD))),
        [VMEM] * 3,
        "mix",
        10**6,
        2**19,
    )(k3, k4, g4)
    g2 = lax.ppermute(two, "ctx", z_route(2))
    g3 = lax.ppermute(two, "ctx", z_route(3))
    g1 = lax.ppermute(one, "ctx", z_route(1))

    q3, c1, c2, c3 = after(q3, c1, c2, c3)
    back = shape((32, 3 * HD))
    s0, s1, s2, s3 = call(
        far_kernel,
        (back,) * 4,
        [VMEM] * 7,
        "far",
        10**9,
        4 * 2**20,
        scratch=[pltpu.VMEM((4, 128, HD), F32)],
    )(q3, q4, q5, g4, g1, g2, g3)
    _, w_other = after(s1, w_other)
    w_pair = lax.ppermute(w_other, "head", core_route())
    b1 = lax.ppermute(s1, "ctx", x_route(1))
    b3 = lax.ppermute(s3, "ctx", x_route(3))
    b2 = lax.ppermute(s2, "ctx", x_route(2))

    _, q1, *leaf = after(s1, q1, *leaf)
    leaf = call(
        home_kernel,
        (shape((4, LEAF, HD), F32),) * 3,
        [VMEM] * 8,
        "home",
        2 * 10**9,
        4 * 2**20,
        scratch=[pltpu.VMEM((4, 256, HD), F32)],
    )(q1, q2, c1, c2, c3, *leaf)

    rows = 2 * LEAF
    mine = call(
        finish_kernel,
        shape((rows, 4 * HD)),
        [VMEM] * 7,
        "finish",
        10**8,
        3 * 2**20,
        scratch=[pltpu.VMEM((4, 256, HD), F32)],
    )(s0, b1, b2, b3, *leaf)
    pair = lax.ppermute(mine, "head", core_route())
    part = call(
        begin_kernel,
        shape((NY, 512, rows), F32),
        [VMEM] * 2,
        "chunk_begin",
        10**9,
        6 * 2**20,
    )(w_mine, mine)

    def chunk(j):
        return pl.BlockSpec((1, 512, 512), lambda i, j=j: (j, 0, 0))

    whole = pl.BlockSpec((rows, 4 * HD), lambda i: (0, 0))
    half = pl.BlockSpec((256, rows), lambda i: (0, 0))
    full = pl.BlockSpec((512, rows), lambda i: (0, 0))
    far_a, far_b = call(
        far_chunk_kernel,
        (shape((256, rows)),) * 2,
        [chunk(2)] * 2 + [whole],
        "chunk_far",
        5 * 10**8,
        2 * 2**20,
        out_specs=(half,) * 2,
        grid=(1,),
    )(w_pair, part, pair)
    got_a = lax.ppermute(far_a, "head", y_route(1))
    got_b = lax.ppermute(far_b, "head", y_route(3))
    _, part2, pair2 = after(far_a, part, pair)
    up_b, down_a = call(
        near_chunk_kernel,
        (shape((256, rows)),) * 2,
        [chunk(1), chunk(3)] * 2 + [whole],
        "chunk_near",
        5 * 10**8,
        3 * 2**20,
        out_specs=(half,) * 2,
        grid=(1,),
    )(w_pair, w_pair, part2, part2, pair2)
    from_down_b = lax.ppermute(up_b, "head", y_route(1))
    from_up_a = lax.ppermute(down_a, "head", y_route(3))
    _, part3, pair3 = after(up_b, part, pair)
    up_a, down_b, own = call(
        own_chunk_kernel,
        (shape((256, rows), F32),) * 2 + (shape((512, rows), F32),),
        [chunk(1), chunk(3), chunk(0)] * 2 + [whole],
        "chunk_own",
        10**9,
        5 * 2**20,
        out_specs=(half, half, full),
        grid=(1,),
    )(w_pair, w_pair, w_pair, part3, part3, part3, pair3)
    send_up, send_down = call(
        relay_kernel, (shape((256, rows)),) * 2, [VMEM] * 4, "relay", 10**6, 2 * 2**20
    )(up_a, got_a, down_b, got_b)
    from_down_a = lax.ppermute(send_up, "head", y_route(1))
    from_up_b = lax.ppermute(send_down, "head", y_route(3))
    return call(
        total_kernel,
        (shape((512, LEAF)),) * 2,
        [VMEM] * 5,
        "total",
        10**6,
        3 * 2**20,
    )(own, from_down_a, from_up_a, from_down_b, from_up_b)


def solution(mesh):
    return jax.shard_map(
        on_device,
        mesh=mesh,
        in_specs=(P("ctx", "head"),) * 6 + (P("head", None),),
        out_specs=(P("head", "ctx"), P("head", "ctx")),
        check_vma=False,
    )
```
